512 devices in a mesh: row: 64 (over z, y_hi, core), col: 8 (over y_lo, x).
Axes of the slice: x: 4, y: 8 (y_hi: 4, y_lo: 2; y = y_hi * 2 + y_lo), z: 8, core: 2. Of those that a mesh axis runs over, the one named last changes fastest.
Arguments:
- left_projection: bfloat16 [128, 512, 32], P('col', 'row'), may hold values from -6 to 6
- right_projection: bfloat16 [128, 512, 32], P('row', 'col'), may hold values from -6 to 6
- output_weight: bfloat16 [1024, 128], replicated, may hold values from -0.1875 to 0.1875
- pair_update_gradient: bfloat16 [512, 512, 128], P('row', 'col'), may hold values from -6 to 6
- alignment_mask: int32 [128, 512], replicated, may hold values from 0 to 1, as said below
Outputs:
- first_factor_derivative: bfloat16 [128, 512, 32], P('col', 'row')
- grad_right: bfloat16 [128, 512, 32], P('row', 'col')
- grad_wout: float32 [1024, 128], replicated
- grad_bias: float32 [128], replicated
The draws below stay inside these ranges and needn't reach their ends.
Inputs may be any that keep to these rules, and one draw needn't show every extreme that they name: `alignment_mask`: the last residues of the crop, from 1 to 4 of them, are 0 in every 128 row.
All inputs are finite; a program needn't handle non-finite values.
Results may differ from the reference program's by a relative error of at most 0.0058.
Values may be sent and summed in bfloat16 or wider, within the bound.
No kernel may reach another device: no remote copies, remote signals or barrier semaphores. Data moves between devices by JAX's collectives and lax.ppermute only.
A program may use at most 64 MiB of HBM per device.

```python
import jax
import jax.numpy as jnp
from jax import lax

HIDDEN_FEATURES = 32
PAIR_CHANNELS = 128
SEQUENCE_COUNT = 128
RES_DEV = 8
OUTER_CHANNELS = 1024
WINDOW_LENGTH = 512


def draw_alignment_mask(key, part):
    key_pad, random_key_rows, random_key_gaps = jax.random.split(jax.random.fold_in(key, 11), 3)
    padding = jax.random.randint(key_pad, (), 1, RES_DEV // 2 + 1)
    position = jnp.arange(WINDOW_LENGTH, dtype=jnp.int32)[None, :]
    residue_live = position < WINDOW_LENGTH - padding
    row_present = jax.random.randint(random_key_rows, (SEQUENCE_COUNT, 1), 0, 16) != 0
    kept_fraction = jax.random.randint(random_key_gaps, (SEQUENCE_COUNT, WINDOW_LENGTH), 0, 8) != 0
    return (residue_live & row_present & kept_fraction).astype(jnp.int32)


def levels(own_key, extent, cuts, smallest, high):
    loudness, own = 1.0, jax.random.fold_in(own_key, 6)
    for axis_at, blocks in cuts:
        steps = jnp.exp(jax.random.uniform(jax.random.fold_in(own, axis_at), (blocks,), jnp.float32, smallest / len(cuts), high / len(cuts)))
        loudness = loudness * jnp.repeat(steps, extent[axis_at] // blocks).reshape([-1 if axis == axis_at else 1 for axis in range(len(extent))])
    return loudness


def gaussian(own_key, shape, width, most, shards=(), kind=jnp.bfloat16):
    result = jax.random.normal(own_key, shape, jnp.float32) * width
    if len(shards) > 0:
        result = levels(own_key, shape, shards, -0.22, 0.18) * result
    return jnp.clip(result, min=-most, max=most).astype(kind)


def setup_inputs(seed: int = 0) -> dict:
    seeds = jax.random.split(jax.random.key(seed), 6)
    return {
        "left_projection": gaussian(seeds[0], (SEQUENCE_COUNT, WINDOW_LENGTH, HIDDEN_FEATURES), 1.0, 6.0, ((0, 8), (1, 64))),
        "right_projection": gaussian(seeds[1], (SEQUENCE_COUNT, WINDOW_LENGTH, HIDDEN_FEATURES), 1.0, 6.0, ((0, 64), (1, 8))),
        "output_weight": gaussian(seeds[2], (OUTER_CHANNELS, PAIR_CHANNELS), OUTER_CHANNELS ** -0.5, 0.1875),
        "pair_update_gradient": gaussian(seeds[3], (WINDOW_LENGTH, WINDOW_LENGTH, PAIR_CHANNELS), 1.0, 6.0, ((0, 64), (1, 8))),
        "alignment_mask": draw_alignment_mask(jax.random.fold_in(seeds[5], 71), 0),
    }


def reference(left_projection, right_projection, output_weight, pair_update_gradient, alignment_mask):
    presence_indicator_real = alignment_mask.astype(jnp.float32)
    mask_boolean = alignment_mask.astype(jnp.bfloat16)
    counts = jnp.dot(presence_indicator_real.T, presence_indicator_real, preferred_element_type=jnp.float32)
    masked_left_rows = left_projection * mask_boolean[:, :, None]
    right_masked = right_projection * mask_boolean[:, :, None]
    right_wide = right_masked.astype(jnp.float32)
    rows_per_block = 8
    number_of_blocks = WINDOW_LENGTH // rows_per_block

    def block_step(totals, index):
        weight_sum, bias_sum, right_sum = totals
        begin_at = index * rows_per_block
        pair_block = lax.dynamic_slice_in_dim(pair_update_gradient, begin_at, rows_per_block, 0)
        count_block = lax.dynamic_slice_in_dim(counts, begin_at, rows_per_block, 0)
        scaled_f = pair_block.astype(jnp.float32) / jnp.maximum(count_block, 1.0)[:, :, None]
        bias_sum = bias_sum + jnp.sum(scaled_f, axis=(0, 1))
        scaled = scaled_f.astype(jnp.bfloat16)
        pair_flat = scaled.reshape(rows_per_block * WINDOW_LENGTH, PAIR_CHANNELS)
        grad_outer = jnp.dot(pair_flat, output_weight.T, preferred_element_type=jnp.float32).astype(jnp.bfloat16)
        grad_wide = grad_outer.astype(jnp.float32).reshape(rows_per_block, WINDOW_LENGTH, HIDDEN_FEATURES, HIDDEN_FEATURES)
        left_block = lax.dynamic_slice_in_dim(masked_left_rows, begin_at, rows_per_block, 1).astype(jnp.float32)
        outer_tile = jnp.einsum("sic,sjd->ijcd", left_block, right_wide).astype(jnp.bfloat16)
        weight_sum = weight_sum + jnp.dot(outer_tile.reshape(rows_per_block * WINDOW_LENGTH, OUTER_CHANNELS).T, pair_flat, preferred_element_type=jnp.float32)
        left_grad = jnp.einsum("ijcd,sjd->sic", grad_wide, right_wide)
        right_sum = right_sum + jnp.einsum("ijcd,sic->sjd", grad_wide, left_block)
        return (weight_sum, bias_sum, right_sum), left_grad

    starting_carry = (jnp.zeros((OUTER_CHANNELS, PAIR_CHANNELS), jnp.float32), jnp.zeros((PAIR_CHANNELS,), jnp.float32), jnp.zeros((SEQUENCE_COUNT, WINDOW_LENGTH, HIDDEN_FEATURES), jnp.float32))
    totals, first_factor_portions = lax.scan(block_step, starting_carry, jnp.arange(number_of_blocks, dtype=jnp.int32))
    weight_sum, bias_sum, right_sum = totals
    first_factor_summands = first_factor_portions.transpose(1, 0, 2, 3).reshape(SEQUENCE_COUNT, WINDOW_LENGTH, HIDDEN_FEATURES)
    first_factor_derivative = (first_factor_summands * presence_indicator_real[:, :, None]).astype(jnp.bfloat16)
    grad_right = (right_sum * presence_indicator_real[:, :, None]).astype(jnp.bfloat16)
    return first_factor_derivative, grad_right, weight_sum, bias_sum
```

```python
import jax
import jax.numpy as jnp
from jax import lax
from jax.experimental import pallas as pl
from jax.experimental.pallas import tpu as pltpu
from jax.sharding import Mesh
from jax.sharding import PartitionSpec as P

SHAPE = (8, 4, 2, 2, 4)
NAMES = ("z", "yh", "core", "yl", "x")
ROW = ("z", "yh", "core")
ZY = ("z", "yh")
COL = ("yl", "x")
CHIP_COL = ("core", "yl", "x")
C = 32
K = 128
S = 128
TI, TJ = 16, 32
F32, BF16 = jnp.float32, jnp.bfloat16
VMEM = pl.BlockSpec(memory_space=pltpu.VMEM)


def dot(a, b, ca, cb):
    return lax.dot_general(a, b, (((ca,), (cb,)), ((), ())), preferred_element_type=F32)


def scale_kernel(pair_ref, mi_ref, mj_ref, w_ref, s_ref, bias_ref, g_ref):
    live = mi_ref[...][:, None, :] * mj_ref[...][None, :, :]
    live = live.reshape(TI * TJ, S).astype(BF16)
    counts = dot(live, jnp.ones((S, K), BF16), 1, 0)
    scaled = pair_ref[...].reshape(TI * TJ, K).astype(F32) / jnp.maximum(counts, 1.0)
    total = jnp.sum(scaled, axis=0, keepdims=True)
    high = total.astype(BF16).astype(F32)
    row = lax.broadcasted_iota(jnp.int32, (8, K), 0)
    bias_ref[...] = jnp.where(row == 0, high, jnp.where(row == 1, total - high, 0.0)).astype(BF16)
    scaled = scaled.astype(BF16)
    s_ref[...] = scaled
    for g in range(C // 4):
        part = dot(w_ref[g * 4 * C : (g + 1) * 4 * C, :], scaled, 1, 1).astype(BF16)
        for i in range(TI):
            g_ref[i * C : (i + 1) * C, g * K : (g + 1) * K] = jnp.concatenate(
                [part[e * C : (e + 1) * C, i * TJ : (i + 1) * TJ] for e in range(4)], axis=1
            )


def main_kernel(l_ref, r_ref, s_ref, g_ref, left_ref, right_ref, wout_ref, o_ref):
    left = jnp.concatenate([l_ref[0], l_ref[1]], axis=1)
    right = r_ref[...]
    o_ref[...] = dot(left, right, 0, 0).astype(BF16)
    pairs = s_ref[...]
    for g in range(C // 4):
        rows = []
        for e in range(4):
            at = g * K + e * TJ
            rows.append(
                jnp.concatenate(
                    [o_ref[i * C : (i + 1) * C, at : at + TJ] for i in range(TI)], axis=1
                )
            )
        outer = jnp.concatenate(rows, axis=0)
        wout_ref[g * 4 * C : (g + 1) * 4 * C, :] = dot(outer, pairs, 1, 0).astype(BF16)
    grad = g_ref[...]
    right_ref[...] = dot(left, grad, 1, 0).astype(BF16)
    left_ref[...] = dot(right, grad, 1, 1).astype(BF16)


def per_device(left, right, weight, pair, mask):
    row_at = lax.axis_index(ROW)
    zy_at = lax.axis_index(ZY)
    col_at = lax.axis_index(COL)
    core_at = lax.axis_index("core")
    pair = lax.all_to_all(pair.reshape(8, 2, TJ, K), "core", 1, 0, tiled=True)
    pair = pair.reshape(2, 8, TJ, K).reshape(TI, TJ, K)
    mask_i = lax.dynamic_slice_in_dim(mask, zy_at * TI, TI, 1).T.astype(F32)
    mask_j = lax.dynamic_slice_in_dim(mask, col_at * 64 + core_at * TJ, TJ, 1).T.astype(F32)
    weight = weight.reshape(C, C, K).transpose(1, 0, 2).reshape(C * C, K)
    right_mask = lax.dynamic_slice(mask, (row_at * 2, col_at * 64), (2, 64)).astype(BF16)
    send = (right * right_mask[:, :, None]).transpose(0, 2, 1).reshape(2, C, 2, TJ)
    send = send.transpose(2, 0, 1, 3).reshape(1, 2, 2, C * TJ)
    send = jnp.broadcast_to(send, (32, 2, 2, C * TJ)).reshape(64, 2, C * TJ)
    right_all = lax.all_to_all(send, ROW, 0, 0, tiled=True).reshape(S, C * TJ)
    left_mask = lax.dynamic_slice(mask, (col_at * 16, row_at * 8), (16, 8)).astype(BF16)
    send = (left * left_mask[:, :, None]).reshape(1, 16, 8 * C)
    send = jnp.broadcast_to(send, (16, 16, 8 * C))
    left_all = lax.all_to_all(send, CHIP_COL, 0, 0, tiled=True).reshape(2, S, 8 * C)

    scaled, bias, grad = pl.pallas_call(
        scale_kernel,
        out_shape=(
            jax.ShapeDtypeStruct((TI * TJ, K), BF16),
            jax.ShapeDtypeStruct((8, K), BF16),
            jax.ShapeDtypeStruct((TI * C, C * TJ), BF16),
        ),
        in_specs=[VMEM] * 4,
        out_specs=(VMEM,) * 3,
        compiler_params=pltpu.CompilerParams(vmem_limit_bytes=32 << 20),
        cost_estimate=pl.CostEstimate(flops=150_000_000, bytes_accessed=2_000_000, transcendentals=0),
    )(pair, mask_i, mask_j, weight)
    left_part, right_part, wout_part = pl.pallas_call(
        main_kernel,
        out_shape=(
            jax.ShapeDtypeStruct((S, TI * C), BF16),
            jax.ShapeDtypeStruct((S, C * TJ), BF16),
            jax.ShapeDtypeStruct((C * C, K), BF16),
        ),
        in_specs=[VMEM] * 4,
        out_specs=(VMEM,) * 3,
        scratch_shapes=[pltpu.VMEM((TI * C, C * TJ), BF16)],
        compiler_params=pltpu.CompilerParams(vmem_limit_bytes=32 << 20),
        cost_estimate=pl.CostEstimate(flops=600_000_000, bytes_accessed=3_000_000, transcendentals=0),
    )(left_all, right_all, scaled, grad)

    send = jnp.concatenate(
        [
            right_part.reshape(64, 16, K),
            wout_part.reshape(64, 16, K),
            jnp.broadcast_to(bias[None], (64, 8, K)),
        ],
        axis=1,
    )
    got = lax.all_to_all(send, ROW, 0, 0, tiled=True).astype(F32).reshape(32, 2, 40, K)
    total = jnp.sum(got[:, :, 16:], axis=(0, 1))
    right_sum = jnp.sum(got[:, :, :16], axis=0).reshape(2, 2, C, TJ)
    right_grad = right_sum.transpose(1, 0, 3, 2).reshape(2, 64, C)
    right_grad = (right_grad * right_mask.astype(F32)[:, :, None]).astype(BF16)
    bias_sum = total[16] + total[17]
    high = lax.reduce_precision(bias_sum, 8, 7)
    bias_rows = jnp.concatenate([high[None], (bias_sum - high)[None], jnp.zeros((6, K), F32)])
    left_send = left_part.reshape(8, 16, 2, 8 * C).transpose(2, 0, 1, 3).reshape(16, 32, K)
    rows = jnp.concatenate([total[:16], bias_rows]).astype(BF16)
    send = jnp.concatenate([left_send, jnp.broadcast_to(rows[None], (16, 24, K))], axis=1)
    got = lax.all_to_all(send, CHIP_COL, 0, 0, tiled=True).astype(F32)
    left_grad = jnp.sum(got[:, :32], axis=0).reshape(16, 8, C)
    left_grad = (left_grad * left_mask.astype(F32)[:, :, None]).astype(BF16)
    bias_sum = jnp.sum(got[:, 48:50], axis=(0, 1)) * 0.5
    rows = jnp.sum(got[:, 32:48].reshape(2, 8, 16, K), axis=1).reshape(1, 32, K).astype(BF16)
    wout = lax.all_to_all(jnp.broadcast_to(rows, (32, 32, K)), ZY, 0, 0, tiled=True)
    wout = wout.reshape(C, C, K).transpose(1, 0, 2).reshape(C * C, K).astype(F32)
    return left_grad, right_grad, wout, bias_sum


def solution(mesh):
    parts = Mesh(mesh.devices.reshape(SHAPE), NAMES)
    left_spec, right_spec = P(COL, ROW, None), P(ROW, COL, None)
    return jax.shard_map(
        per_device,
        mesh=parts,
        in_specs=(left_spec, right_spec, P(), P(ROW, COL, None), P()),
        out_specs=(left_spec, right_spec, P(), P()),
        check_vma=False,
    )
```

```python
import jax
import jax.numpy as jnp
from jax import lax
from jax.experimental import pallas as pl
from jax.experimental.pallas import tpu as pltpu
from jax.sharding import Mesh
from jax.sharding import PartitionSpec as P

SHAPE = (4, 2, 4, 2, 2, 4)
NAMES = ("zq", "zb", "yh", "core", "yl", "x")
ROW = ("zq", "zb", "yh", "core")
ZY = ("zq", "zb", "yh")
COL = ("yl", "x")
NEAR = ("zb", "core", "yl", "x")
FAR = ("zq", "yh")
C = 32
K = 128
S = 128
TI, TJ = 16, 32
F32, BF16 = jnp.float32, jnp.bfloat16
VMEM = pl.BlockSpec(memory_space=pltpu.VMEM)
SMEM = pl.BlockSpec(memory_space=pltpu.SMEM)


def dot(a, b, ca, cb):
    return lax.dot_general(a, b, (((ca,), (cb,)), ((), ())), preferred_element_type=F32)


def scale_kernel(
    at_ref, keep_ref, take_ref, m_ref, mi_ref, mj_ref, w_ref, l_in,
    s_ref, bias_ref, g_ref, l_ref, rkeep_ref, rgive_ref, right_ref,
):
    keep, take = keep_ref[...], take_ref[...]
    first = at_ref[0] == 0
    pair = jnp.concatenate([jnp.where(first, keep, take), jnp.where(first, take, keep)])
    live = mi_ref[...][:, None, :] * mj_ref[...][None, :, :]
    live = live.reshape(TI * TJ, S).astype(BF16)
    counts = dot(live, jnp.ones((S, K), BF16), 1, 0)
    scaled = pair.reshape(TI * TJ, K).astype(F32) / jnp.maximum(counts, 1.0)
    total = jnp.sum(scaled, axis=0, keepdims=True)
    high = total.astype(BF16).astype(F32)
    row = lax.broadcasted_iota(jnp.int32, (8, K), 0)
    bias_ref[...] = jnp.where(row == 0, high, jnp.where(row == 1, total - high, 0.0)).astype(BF16)
    scaled = scaled.astype(BF16)
    s_ref[...] = scaled
    for g in range(C // 4):
        part = dot(w_ref[g * 4 * C : (g + 1) * 4 * C, :], scaled, 1, 1).astype(BF16)
        for i in range(TI):
            g_ref[i * C : (i + 1) * C, g * K : (g + 1) * K] = jnp.concatenate(
                [part[e * C : (e + 1) * C, i * TJ : (i + 1) * TJ] for e in range(4)], axis=1
            )
    lane = lax.broadcasted_iota(jnp.int32, (TI, TI * C), 1) // C
    spread = (lane == lax.broadcasted_iota(jnp.int32, (TI, TI * C), 0)).astype(BF16)
    live = dot(m_ref[...], spread, 1, 0).astype(BF16)
    for core in range(2):
        lanes = slice(core * 8 * C, (core + 1) * 8 * C)
        for col in range(8):
            rows = slice(col * 16, (col + 1) * 16)
            l_ref[rows, lanes] = l_in[core * 8 + col] * live[rows, lanes]
    right_ref[...] = dot(l_ref[...], g_ref[...], 1, 0).astype(BF16)
    zb = at_ref[1]
    for zq in range(4):
        at = zq * 32 + zb * 16
        rkeep_ref[zq] = right_ref[pl.ds(pl.multiple_of(at, 16), 16), :]
        at = zq * 32 + (1 - zb) * 16
        rgive_ref[zq] = right_ref[pl.ds(pl.multiple_of(at, 16), 16), :]


def main_kernel(
    l_ref, r_ref, m_ref, s_ref, g_ref, rkeep_ref, rtake_ref, left_ref, wout_ref, rsum_ref, o_ref, w_ref
):
    rsum_ref[...] = (rkeep_ref[...].astype(F32) + rtake_ref[...].astype(F32)).astype(BF16)
    right = r_ref[...] * jnp.concatenate([m_ref[...]] * C, axis=1)
    o_ref[...] = dot(l_ref[...], right, 0, 0).astype(BF16)
    pairs = s_ref[...]
    for g in range(C // 4):
        rows = []
        for e in range(4):
            at = g * K + e * TJ
            rows.append(
                jnp.concatenate(
                    [o_ref[i * C : (i + 1) * C, at : at + TJ] for i in range(TI)], axis=1
                )
            )
        outer = jnp.concatenate(rows, axis=0)
        w_ref[g * 4 * C : (g + 1) * 4 * C, :] = dot(outer, pairs, 1, 0)
    for c in range(C):
        wout_ref[c * C : (c + 1) * C, :] = w_ref[pl.ds(c, C, stride=C), :].astype(BF16)
    left_ref[...] = dot(right, g_ref[...], 1, 1).astype(BF16)


def turn(x, axis, by):
    n = SHAPE[NAMES.index(axis)]
    return lax.ppermute(x, axis, [(i, (i + by) % n) for i in range(n)])


def per_device(left, right, weight, pair, mask):
    row_at = lax.axis_index(ROW)
    zy_at = lax.axis_index(ZY)
    col_at = lax.axis_index(COL)
    core_at = lax.axis_index("core")
    zb_at = lax.axis_index("zb")
    send = jnp.broadcast_to(left.reshape(1, 16, 8 * C), (16, 16, 8 * C))
    left_all = lax.all_to_all(send, ("core",) + COL, 0, 0, tiled=True)
    send = right.transpose(0, 2, 1).reshape(2, C, 2, TJ)
    send = send.transpose(2, 0, 1, 3).reshape(1, 2, 2, C * TJ)
    send = jnp.broadcast_to(send, (32, 2, 2, C * TJ)).reshape(64, 2, C * TJ)
    right_all = lax.all_to_all(send, ROW, 0, 0, tiled=True).reshape(S, C * TJ)
    keep = lax.dynamic_slice_in_dim(pair, core_at * TJ, TJ, 1)
    give = lax.dynamic_slice_in_dim(pair, (1 - core_at) * TJ, TJ, 1)
    take = turn(give, "core", 1)
    mask_i = lax.dynamic_slice_in_dim(mask, zy_at * TI, TI, 1)
    mask_j = lax.dynamic_slice_in_dim(mask, col_at * 64 + core_at * TJ, TJ, 1)
    weight = weight.reshape(C, C, K).transpose(1, 0, 2).reshape(C * C, K)
    at = jnp.stack([core_at, zb_at]).astype(jnp.int32)

    scaled, bias, grad, left_all, right_keep, right_give = pl.pallas_call(
        scale_kernel,
        out_shape=(
            jax.ShapeDtypeStruct((TI * TJ, K), BF16),
            jax.ShapeDtypeStruct((8, K), BF16),
            jax.ShapeDtypeStruct((TI * C, C * TJ), BF16),
            jax.ShapeDtypeStruct((S, TI * C), BF16),
            jax.ShapeDtypeStruct((4, 16, C * TJ), BF16),
            jax.ShapeDtypeStruct((4, 16, C * TJ), BF16),
        ),
        in_specs=[SMEM] + [VMEM] * 7,
        out_specs=(VMEM,) * 6,
        scratch_shapes=[pltpu.VMEM((S, C * TJ), BF16)],
        compiler_params=pltpu.CompilerParams(vmem_limit_bytes=32 << 20),
        cost_estimate=pl.CostEstimate(flops=300_000_000, bytes_accessed=3_000_000, transcendentals=0),
    )(
        at, keep, take, mask_i.astype(BF16), mask_i.T.astype(F32), mask_j.T.astype(F32), weight, left_all
    )
    left_part, wout_part, right_part = pl.pallas_call(
        main_kernel,
        out_shape=(
            jax.ShapeDtypeStruct((S, TI * C), BF16),
            jax.ShapeDtypeStruct((C * C, K), BF16),
            jax.ShapeDtypeStruct((4, 16, C * TJ), BF16),
        ),
        in_specs=[VMEM] * 7,
        out_specs=(VMEM,) * 3,
        scratch_shapes=[pltpu.VMEM((TI * C, C * TJ), BF16), pltpu.VMEM((C * C, K), F32)],
        compiler_params=pltpu.CompilerParams(vmem_limit_bytes=32 << 20),
        cost_estimate=pl.CostEstimate(flops=450_000_000, bytes_accessed=3_000_000, transcendentals=0),
    )(left_all, right_all, mask_j.astype(BF16), scaled, grad, right_keep, turn(right_give, "zb", 1))

    left_send = left_part.reshape(8, 16, 2, 8 * C).transpose(2, 0, 1, 3).reshape(1, 16, 32, K)
    send = jnp.concatenate(
        [
            jnp.broadcast_to(left_send, (2, 16, 32, K)).reshape(32, 32, K),
            wout_part.reshape(32, 32, K),
            jnp.broadcast_to(bias[None], (32, 8, K)),
        ],
        axis=1,
    )
    got = lax.all_to_all(send, NEAR, 0, 0, tiled=True)
    total = jnp.sum(got[:, 32:].astype(F32), axis=0)
    left_got = lax.dynamic_slice_in_dim(got, zb_at * 16, 16, 0)[:, :32]
    left_grad = jnp.sum(left_got.astype(F32), axis=0).reshape(16, 8, C)
    left_mask = lax.dynamic_slice(mask, (col_at * 16, row_at * 8), (16, 8))
    left_grad = (left_grad * left_mask.astype(F32)[:, :, None]).astype(BF16)
    bias_sum = total[32] + total[33]
    high = lax.reduce_precision(bias_sum, 8, 7)
    bias_rows = jnp.concatenate([high[None], (bias_sum - high)[None], jnp.zeros((6, K), F32)])
    rows = jnp.concatenate([total[:32], bias_rows]).astype(BF16)
    send = jnp.concatenate(
        [right_part.reshape(16, 32, K), jnp.broadcast_to(rows[None], (16, 40, K))], axis=1
    )
    got = lax.all_to_all(send, FAR, 0, 0, tiled=True).astype(F32)
    total = jnp.sum(got, axis=0)
    bias_sum = total[64] + total[65]
    right_sum = total[:32].reshape(1, 2, 1, 16, K).astype(BF16)
    rows = total[32:64].reshape(1, 1, 1, 32, K).astype(BF16)
    send = jnp.concatenate(
        [jnp.broadcast_to(rows, (2, 2, 8, 32, K)), jnp.broadcast_to(right_sum, (2, 2, 8, 16, K))], axis=3
    )
    got = lax.all_to_all(send.reshape(32, 48, K), NEAR, 0, 0, tiled=True)
    wout = got[:, :32].reshape(C * C, K).astype(F32)
    right_grad = lax.dynamic_slice(got.reshape(2, 2, 8, 48, K), (zb_at, 0, col_at, 32, 0), (1, 2, 1, 16, K))
    right_grad = right_grad.reshape(2, 2, C, TJ)
    right_mask = lax.dynamic_slice(mask, (row_at * 2, col_at * 64), (2, 64)).astype(BF16)
    right_grad = right_grad.transpose(1, 0, 3, 2).reshape(2, 64, C) * right_mask[:, :, None]
    return left_grad, right_grad, wout, bias_sum


def solution(mesh):
    parts = Mesh(mesh.devices.reshape(SHAPE), NAMES)
    left_spec, right_spec = P(COL, ROW, None), P(ROW, COL, None)
    return jax.shard_map(
        per_device,
        mesh=parts,
        in_specs=(left_spec, right_spec, P(), P(ROW, COL, None), P()),
        out_specs=(left_spec, right_spec, P(), P()),
        check_vma=False,
    )
```

```python
import jax
import jax.numpy as jnp
from jax import lax
from jax.experimental import pallas as pl
from jax.experimental.pallas import tpu as pltpu
from jax.sharding import Mesh
from jax.sharding import PartitionSpec as P

SHAPE = (4, 2, 4, 2, 2, 4)
NAMES = ("zq", "zb", "yh", "core", "yl", "x")
ROW = ("zq", "zb", "yh", "core")
ZY = ("zq", "zb", "yh")
COL = ("yl", "x")
NEAR = ("zb", "core", "yl", "x")
FAR = ("zq", "yh")
C = 32
K = 128
S = 128
TI, TJ = 16, 32
F32, BF16 = jnp.float32, jnp.bfloat16
VMEM = pl.BlockSpec(memory_space=pltpu.VMEM)
SMEM = pl.BlockSpec(memory_space=pltpu.SMEM)


def dot(a, b, ca, cb):
    return lax.dot_general(a, b, (((ca,), (cb,)), ((), ())), preferred_element_type=F32)


def copies_kernel(l_ref, send_ref):
    left = l_ref[...].astype(F32)
    left = jnp.concatenate([left[:, i, :] for i in range(8)], axis=1).astype(BF16)
    for to in range(16):
        send_ref[to] = left


def scale_kernel(
    at_ref, keep_ref, take_ref, m_ref, mi_ref, mj_ref, w_ref, l_in,
    s_ref, bias_ref, g_ref, l_ref, rkeep_ref, rgive_ref, right_ref,
):
    keep, take = keep_ref[...], take_ref[...]
    first = at_ref[0] == 0
    pair = jnp.concatenate([jnp.where(first, keep, take), jnp.where(first, take, keep)])
    live = mi_ref[...][:, None, :] * mj_ref[...][None, :, :]
    live = live.reshape(TI * TJ, S).astype(BF16)
    counts = dot(live, jnp.ones((S, K), BF16), 1, 0)
    scaled = pair.reshape(TI * TJ, K).astype(F32) / jnp.maximum(counts, 1.0)
    total = jnp.sum(scaled, axis=0, keepdims=True)
    high = total.astype(BF16).astype(F32)
    row = lax.broadcasted_iota(jnp.int32, (16, K), 0)
    bias_ref[...] = jnp.where(row == 0, high, jnp.where(row == 1, total - high, 0.0)).astype(BF16)
    scaled = scaled.astype(BF16)
    s_ref[...] = scaled
    for g in range(C // 4):
        part = dot(w_ref[g * 4 * C : (g + 1) * 4 * C, :], scaled, 1, 1).astype(BF16)
        for i in range(TI):
            g_ref[i * C : (i + 1) * C, g * K : (g + 1) * K] = jnp.concatenate(
                [part[e * C : (e + 1) * C, i * TJ : (i + 1) * TJ] for e in range(4)], axis=1
            )
    lane = lax.broadcasted_iota(jnp.int32, (TI, TI * C), 1) // C
    spread = (lane == lax.broadcasted_iota(jnp.int32, (TI, TI * C), 0)).astype(BF16)
    live = dot(m_ref[...], spread, 1, 0).astype(BF16)
    for core in range(2):
        lanes = slice(core * 8 * C, (core + 1) * 8 * C)
        for col in range(8):
            rows = slice(col * 16, (col + 1) * 16)
            l_ref[rows, lanes] = l_in[core * 8 + col] * live[rows, lanes]
    right_ref[...] = dot(l_ref[...], g_ref[...], 1, 0).astype(BF16)
    zb = at_ref[1]
    for zq in range(4):
        at = zq * 32 + zb * 16
        rkeep_ref[zq] = right_ref[pl.ds(pl.multiple_of(at, 16), 16), :]
        at = zq * 32 + (1 - zb) * 16
        rgive_ref[zq] = right_ref[pl.ds(pl.multiple_of(at, 16), 16), :]


def main_kernel(
    l_ref, r_ref, m_ref, s_ref, g_ref, bias_ref, send_ref, o_ref, w_ref, left_ref
):
    right = r_ref[...] * jnp.concatenate([m_ref[...]] * C, axis=1)
    o_ref[...] = dot(l_ref[...], right, 0, 0).astype(BF16)
    pairs = s_ref[...]
    for g in range(C // 4):
        rows = []
        for e in range(4):
            at = g * K + e * TJ
            rows.append(
                jnp.concatenate(
                    [o_ref[i * C : (i + 1) * C, at : at + TJ] for i in range(TI)], axis=1
                )
            )
        outer = jnp.concatenate(rows, axis=0)
        w_ref[g * 4 * C : (g + 1) * 4 * C, :] = dot(outer, pairs, 1, 0)
    for c in range(C):
        send_ref[c, 32:64, :] = w_ref[pl.ds(c, C, stride=C), :].astype(BF16)
        send_ref[c, 64:80, :] = bias_ref[...]
    left_ref[...] = dot(right, g_ref[...], 1, 1).astype(BF16)
    for zb in range(2):
        for core in range(2):
            for col in range(8):
                for h in range(2):
                    at = core * 8 * C + h * K
                    send_ref[zb * 16 + core * 8 + col, h * 16 : (h + 1) * 16, :] = left_ref[
                        col * 16 : (col + 1) * 16, at : at + K
                    ]


def join_kernel(got_ref, l_ref, ml_ref, send_ref, left_ref, bias_ref):
    total = got_ref[0].astype(F32)
    for source in range(1, 16):
        total = total + got_ref[source].astype(F32)
    bias_ref[...] = total[64:65] + total[65:66]
    rows = total[:64].astype(BF16)
    for zb in range(2):
        for core in range(2):
            for col in range(8):
                to = zb * 16 + core * 8 + col
                send_ref[to, :32, :] = rows[32:64]
                send_ref[to, 32:48, :] = rows[core * 16 : (core + 1) * 16]
    lane = lax.broadcasted_iota(jnp.int32, (8, 8 * C), 1) // C
    spread = (lane == lax.broadcasted_iota(jnp.int32, (8, 8 * C), 0)).astype(BF16)
    left = jnp.concatenate([l_ref[:16, :], l_ref[16:, :]], axis=1)
    left_ref[...] = (left * dot(ml_ref[...], spread, 1, 0)).astype(BF16)


def tail_kernel(at_ref, got_ref, m_ref, wout_ref, right_ref, turned_ref):
    for c in range(C):
        wout_ref[c * C : (c + 1) * C, :] = got_ref[c, :32, :].astype(F32)
    near, far = [got_ref[at_ref[0] + core * 8, 32:48, :].astype(F32) for core in range(2)]
    for q in range(2):
        for e in range(4):
            rows, lanes = slice(q * 8, (q + 1) * 8), slice(e * TJ, (e + 1) * TJ)
            piece = jnp.concatenate([near[rows, lanes], far[rows, lanes]], axis=1)
            turned_ref[q, pl.ds(e, 8, stride=4), :] = piece
    right_ref[...] = (turned_ref[...] * m_ref[...][:, None, :]).astype(BF16)


def turn(x, axis, by):
    n = SHAPE[NAMES.index(axis)]
    return lax.ppermute(x, axis, [(i, (i + by) % n) for i in range(n)])


def per_device(left, right, weight, pair, mask):
    row_at = lax.axis_index(ROW)
    zy_at = lax.axis_index(ZY)
    col_at = lax.axis_index(COL)
    core_at = lax.axis_index("core")
    zb_at = lax.axis_index("zb")
    send = pl.pallas_call(
        copies_kernel,
        out_shape=jax.ShapeDtypeStruct((16, 16, 8 * C), BF16),
        in_specs=[VMEM],
        out_specs=VMEM,
        compiler_params=pltpu.CompilerParams(vmem_limit_bytes=16 << 20),
    )(left)
    left_all = lax.all_to_all(send, ("core",) + COL, 0, 0, tiled=True)
    send = right.transpose(0, 2, 1).reshape(2, C, 2, TJ)
    send = send.transpose(2, 0, 1, 3).reshape(1, 2, 2, C * TJ)
    send = jnp.broadcast_to(send, (32, 2, 2, C * TJ)).reshape(64, 2, C * TJ)
    send, pair = lax.optimization_barrier((send, pair))
    right_all = lax.all_to_all(send, ROW, 0, 0, tiled=True).reshape(S, C * TJ)
    keep = lax.dynamic_slice_in_dim(pair, core_at * TJ, TJ, 1)
    give = lax.dynamic_slice_in_dim(pair, (1 - core_at) * TJ, TJ, 1)
    take = turn(give, "core", 1)
    mask_i = lax.dynamic_slice_in_dim(mask, zy_at * TI, TI, 1)
    mask_j = lax.dynamic_slice_in_dim(mask, col_at * 64 + core_at * TJ, TJ, 1)
    weight = weight.reshape(C, C, K).transpose(1, 0, 2).reshape(C * C, K)
    at = jnp.stack([core_at, zb_at]).astype(jnp.int32)

    scaled, bias, grad, left_all, right_keep, right_give = pl.pallas_call(
        scale_kernel,
        out_shape=(
            jax.ShapeDtypeStruct((TI * TJ, K), BF16),
            jax.ShapeDtypeStruct((16, K), BF16),
            jax.ShapeDtypeStruct((TI * C, C * TJ), BF16),
            jax.ShapeDtypeStruct((S, TI * C), BF16),
            jax.ShapeDtypeStruct((4, 16, C * TJ), BF16),
            jax.ShapeDtypeStruct((4, 16, C * TJ), BF16),
        ),
        in_specs=[SMEM] + [VMEM] * 7,
        out_specs=(VMEM,) * 6,
        scratch_shapes=[pltpu.VMEM((S, C * TJ), BF16)],
        compiler_params=pltpu.CompilerParams(vmem_limit_bytes=32 << 20),
        cost_estimate=pl.CostEstimate(flops=300_000_000, bytes_accessed=3_000_000, transcendentals=0),
    )(
        at, keep, take, mask_i.astype(BF16), mask_i.T.astype(F32), mask_j.T.astype(F32), weight, left_all
    )
    right_take = turn(right_give, "zb", 1)
    right_take, right_all = lax.optimization_barrier((right_take, right_all))
    right_part = (right_keep.astype(F32) + right_take.astype(F32)).astype(BF16)
    send = pl.pallas_call(
        main_kernel,
        out_shape=jax.ShapeDtypeStruct((32, 80, K), BF16),
        in_specs=[VMEM] * 6,
        out_specs=VMEM,
        scratch_shapes=[
            pltpu.VMEM((TI * C, C * TJ), BF16),
            pltpu.VMEM((C * C, K), F32),
            pltpu.VMEM((S, TI * C), BF16),
        ],
        compiler_params=pltpu.CompilerParams(vmem_limit_bytes=32 << 20),
        cost_estimate=pl.CostEstimate(flops=450_000_000, bytes_accessed=3_000_000, transcendentals=0),
    )(left_all, right_all, mask_j.astype(BF16), scaled, grad, bias)

    got = lax.all_to_all(send, NEAR, 0, 0, tiled=True)
    total = jnp.sum(got[:, 32:72].astype(F32), axis=0)
    left_got = lax.dynamic_slice_in_dim(got, zb_at * 16, 16, 0)[:, :32]
    left_sum = jnp.sum(left_got.astype(F32), axis=0)
    left_mask = lax.dynamic_slice(mask, (col_at * 16, row_at * 8), (16, 8)).astype(BF16)
    bias_sum = total[32] + total[33]
    high = lax.reduce_precision(bias_sum, 8, 7)
    bias_rows = jnp.concatenate([high[None], (bias_sum - high)[None], jnp.zeros((6, K), F32)])
    rows = jnp.concatenate([total[:32], bias_rows]).astype(BF16)
    send = jnp.concatenate(
        [right_part.reshape(16, 32, K), jnp.broadcast_to(rows[None], (16, 40, K))], axis=1
    )
    got = lax.all_to_all(send, FAR, 0, 0, tiled=True)
    send, left_grad, bias_sum = pl.pallas_call(
        join_kernel,
        out_shape=(
            jax.ShapeDtypeStruct((32, 48, K), BF16),
            jax.ShapeDtypeStruct((16, 8 * C), BF16),
            jax.ShapeDtypeStruct((1, K), F32),
        ),
        in_specs=[VMEM] * 3,
        out_specs=(VMEM,) * 3,
        compiler_params=pltpu.CompilerParams(vmem_limit_bytes=16 << 20),
    )(got, left_sum, left_mask)
    left_grad = left_grad.reshape(16, 8, C)
    bias_sum = bias_sum.reshape(K)
    got = lax.all_to_all(send, NEAR, 0, 0, tiled=True)
    right_mask = lax.dynamic_slice(mask, (row_at * 2, col_at * 64), (2, 64)).astype(F32)
    at = (zb_at * 16 + col_at).reshape(1).astype(jnp.int32)
    wout, right_grad = pl.pallas_call(
        tail_kernel,
        out_shape=(
            jax.ShapeDtypeStruct((C * C, K), F32),
            jax.ShapeDtypeStruct((2, C, 64), BF16),
        ),
        in_specs=[SMEM] + [VMEM] * 2,
        out_specs=(VMEM,) * 2,
        scratch_shapes=[pltpu.VMEM((2, C, 64), F32)],
        compiler_params=pltpu.CompilerParams(vmem_limit_bytes=16 << 20),
    )(at, got, right_mask)
    right_grad = right_grad.transpose(0, 2, 1)
    return left_grad, right_grad, wout, bias_sum


def solution(mesh):
    parts = Mesh(mesh.devices.reshape(SHAPE), NAMES)
    left_spec, right_spec = P(COL, ROW, None), P(ROW, COL, None)
    return jax.shard_map(
        per_device,
        mesh=parts,
        in_specs=(left_spec, right_spec, P(), P(ROW, COL, None), P()),
        out_specs=(left_spec, right_spec, P(), P()),
        check_vma=False,
    )
```

```python
import jax
import jax.numpy as jnp
from jax import lax
from jax.experimental import pallas as pl
from jax.experimental.pallas import tpu as pltpu
from jax.sharding import Mesh
from jax.sharding import PartitionSpec as P

SHAPE = (4, 2, 4, 2, 2, 4)
NAMES = ("zq", "zb", "yh", "core", "yl", "x")
ROW = ("zq", "zb", "yh", "core")
ZY = ("zq", "zb", "yh")
COL = ("yl", "x")
NEAR = ("zb", "core", "yl", "x")
FAR = ("zq", "yh")
C = 32
K = 128
S = 128
TI, TJ = 16, 32
F32, BF16 = jnp.float32, jnp.bfloat16
VMEM = pl.BlockSpec(memory_space=pltpu.VMEM)
SMEM = pl.BlockSpec(memory_space=pltpu.SMEM)


def dot(a, b, ca, cb):
    return lax.dot_general(a, b, (((ca,), (cb,)), ((), ())), preferred_element_type=F32)


def copies_kernel(l_ref, send_ref):
    left = l_ref[...].astype(F32)
    left = jnp.concatenate([left[:, i, :] for i in range(8)], axis=1).astype(BF16)
    for to in range(16):
        send_ref[to] = left


def scale_kernel(
    at_ref, keep_ref, take_ref, m_ref, mi_ref, mj_ref, w_ref, l_in,
    s_ref, bias_ref, g_ref, l_ref, rkeep_ref, rgive_ref, right_ref,
):
    keep, take = keep_ref[...], take_ref[...]
    first = at_ref[0] == 0
    pair = jnp.concatenate([jnp.where(first, keep, take), jnp.where(first, take, keep)])
    live = mi_ref[...][:, None, :] * mj_ref[...][None, :, :]
    live = live.reshape(TI * TJ, S).astype(BF16)
    counts = dot(live, jnp.ones((S, K), BF16), 1, 0)
    scaled = pair.reshape(TI * TJ, K).astype(F32) / jnp.maximum(counts, 1.0)
    total = jnp.sum(scaled, axis=0, keepdims=True)
    high = total.astype(BF16).astype(F32)
    row = lax.broadcasted_iota(jnp.int32, (16, K), 0)
    bias_ref[...] = jnp.where(row == 0, high, jnp.where(row == 1, total - high, 0.0)).astype(BF16)
    scaled = scaled.astype(BF16)
    s_ref[...] = scaled
    for g in range(C // 4):
        part = dot(w_ref[g * 4 * C : (g + 1) * 4 * C, :], scaled, 1, 1).astype(BF16)
        for i in range(TI):
            g_ref[i * C : (i + 1) * C, g * K : (g + 1) * K] = jnp.concatenate(
                [part[e * C : (e + 1) * C, i * TJ : (i + 1) * TJ] for e in range(4)], axis=1
            )
    lane = lax.broadcasted_iota(jnp.int32, (TI, TI * C), 1) // C
    spread = (lane == lax.broadcasted_iota(jnp.int32, (TI, TI * C), 0)).astype(BF16)
    live = dot(m_ref[...], spread, 1, 0).astype(BF16)
    for core in range(2):
        lanes = slice(core * 8 * C, (core + 1) * 8 * C)
        for col in range(8):
            rows = slice(col * 16, (col + 1) * 16)
            l_ref[rows, lanes] = l_in[core * 8 + col] * live[rows, lanes]
    right_ref[...] = dot(l_ref[...], g_ref[...], 1, 0).astype(BF16)
    zb = at_ref[1]
    for zq in range(4):
        at = zq * 32 + zb * 16
        rkeep_ref[zq] = right_ref[pl.ds(pl.multiple_of(at, 16), 16), :]
        at = zq * 32 + (1 - zb) * 16
        rgive_ref[zq] = right_ref[pl.ds(pl.multiple_of(at, 16), 16), :]


def main_kernel(
    l_ref, r_ref, m_ref, s_ref, g_ref, rkeep_ref, rtake_ref, bias_ref, send_ref, rsum_ref, o_ref, w_ref, left_ref
):
    for zq in range(4):
        total = rkeep_ref[zq].astype(F32) + rtake_ref[zq].astype(F32)
        for yh in range(4):
            rows = [total[yh * 4 : yh * 4 + 4, t * K : (t + 1) * K] for t in range(8)]
            rsum_ref[zq * 4 + yh] = jnp.concatenate(rows, axis=0).astype(BF16)
    right = r_ref[...] * jnp.concatenate([m_ref[...]] * C, axis=1)
    o_ref[...] = dot(l_ref[...], right, 0, 0).astype(BF16)
    pairs = s_ref[...]
    for g in range(C // 4):
        rows = []
        for e in range(4):
            at = g * K + e * TJ
            rows.append(
                jnp.concatenate(
                    [o_ref[i * C : (i + 1) * C, at : at + TJ] for i in range(TI)], axis=1
                )
            )
        outer = jnp.concatenate(rows, axis=0)
        w_ref[g * 4 * C : (g + 1) * 4 * C, :] = dot(outer, pairs, 1, 0)
    for c in range(C):
        send_ref[c, 32:64, :] = w_ref[pl.ds(c, C, stride=C), :].astype(BF16)
        send_ref[c, 64:80, :] = bias_ref[...]
    left_ref[...] = dot(right, g_ref[...], 1, 1).astype(BF16)
    for zb in range(2):
        for core in range(2):
            for col in range(8):
                for h in range(2):
                    at = core * 8 * C + h * K
                    send_ref[zb * 16 + core * 8 + col, h * 16 : (h + 1) * 16, :] = left_ref[
                        col * 16 : (col + 1) * 16, at : at + K
                    ]


def join_kernel(got_ref, send_ref, bias_ref, total_ref):
    total = got_ref[0].astype(F32)
    for source in range(1, 16):
        total = total + got_ref[source].astype(F32)
    bias_ref[...] = total[64:65] + total[65:66]
    rows = total[32:64].astype(BF16)
    total_ref[...] = total[:32]
    for core in range(2):
        right = [total_ref[pl.ds(core * 2 + q, 8, stride=4), :] for q in range(2)]
        right = jnp.concatenate(right, axis=0).astype(BF16)
        for zb in range(2):
            for col in range(8):
                to = zb * 16 + core * 8 + col
                send_ref[to, :32, :] = rows
                send_ref[to, 32:48, :] = right


def left_kernel(l_ref, ml_ref, left_ref):
    lane = lax.broadcasted_iota(jnp.int32, (8, 8 * C), 1) // C
    spread = (lane == lax.broadcasted_iota(jnp.int32, (8, 8 * C), 0)).astype(BF16)
    left = jnp.concatenate([l_ref[:16, :], l_ref[16:, :]], axis=1)
    left_ref[...] = (left * dot(ml_ref[...], spread, 1, 0)).astype(BF16)


def tail_kernel(at_ref, got_ref, m_ref, wout_ref, right_ref, turned_ref):
    for c in range(C):
        wout_ref[c * C : (c + 1) * C, :] = got_ref[c, :32, :].astype(F32)
    near, far = [got_ref[at_ref[0] + core * 8, 32:48, :].astype(F32) for core in range(2)]
    for q in range(2):
        for e in range(4):
            rows, lanes = slice(q * 8, (q + 1) * 8), slice(e * TJ, (e + 1) * TJ)
            piece = jnp.concatenate([near[rows, lanes], far[rows, lanes]], axis=1)
            turned_ref[q, pl.ds(e, 8, stride=4), :] = piece
    right_ref[...] = (turned_ref[...] * m_ref[...][:, None, :]).astype(BF16)


def turn(x, axis, by):
    n = SHAPE[NAMES.index(axis)]
    return lax.ppermute(x, axis, [(i, (i + by) % n) for i in range(n)])


def per_device(left, right, weight, pair, mask):
    row_at = lax.axis_index(ROW)
    zy_at = lax.axis_index(ZY)
    col_at = lax.axis_index(COL)
    core_at = lax.axis_index("core")
    zb_at = lax.axis_index("zb")
    send = pl.pallas_call(
        copies_kernel,
        out_shape=jax.ShapeDtypeStruct((16, 16, 8 * C), BF16),
        in_specs=[VMEM],
        out_specs=VMEM,
        compiler_params=pltpu.CompilerParams(vmem_limit_bytes=16 << 20),
    )(left)
    left_all = lax.all_to_all(send, ("core",) + COL, 0, 0, tiled=True)
    send = right.transpose(0, 2, 1).reshape(2, C, 2, TJ)
    send = send.transpose(2, 0, 1, 3).reshape(1, 2, 2, C * TJ)
    send = jnp.broadcast_to(send, (32, 2, 2, C * TJ)).reshape(64, 2, C * TJ)
    send, pair = lax.optimization_barrier((send, pair))
    right_all = lax.all_to_all(send, ROW, 0, 0, tiled=True).reshape(S, C * TJ)
    keep = lax.dynamic_slice_in_dim(pair, core_at * TJ, TJ, 1)
    give = lax.dynamic_slice_in_dim(pair, (1 - core_at) * TJ, TJ, 1)
    take = turn(give, "core", 1)
    mask_i = lax.dynamic_slice_in_dim(mask, zy_at * TI, TI, 1)
    mask_j = lax.dynamic_slice_in_dim(mask, col_at * 64 + core_at * TJ, TJ, 1)
    weight = weight.reshape(C, C, K).transpose(1, 0, 2).reshape(C * C, K)
    at = jnp.stack([core_at, zb_at]).astype(jnp.int32)

    scaled, bias, grad, left_all, right_keep, right_give = pl.pallas_call(
        scale_kernel,
        out_shape=(
            jax.ShapeDtypeStruct((TI * TJ, K), BF16),
            jax.ShapeDtypeStruct((16, K), BF16),
            jax.ShapeDtypeStruct((TI * C, C * TJ), BF16),
            jax.ShapeDtypeStruct((S, TI * C), BF16),
            jax.ShapeDtypeStruct((4, 16, C * TJ), BF16),
            jax.ShapeDtypeStruct((4, 16, C * TJ), BF16),
        ),
        in_specs=[SMEM] + [VMEM] * 7,
        out_specs=(VMEM,) * 6,
        scratch_shapes=[pltpu.VMEM((S, C * TJ), BF16)],
        compiler_params=pltpu.CompilerParams(vmem_limit_bytes=32 << 20),
        cost_estimate=pl.CostEstimate(flops=300_000_000, bytes_accessed=3_000_000, transcendentals=0),
    )(
        at, keep, take, mask_i.astype(BF16), mask_i.T.astype(F32), mask_j.T.astype(F32), weight, left_all
    )
    send, right_part = pl.pallas_call(
        main_kernel,
        out_shape=(
            jax.ShapeDtypeStruct((32, 80, K), BF16),
            jax.ShapeDtypeStruct((16, 32, K), BF16),
        ),
        in_specs=[VMEM] * 8,
        out_specs=(VMEM,) * 2,
        scratch_shapes=[
            pltpu.VMEM((TI * C, C * TJ), BF16),
            pltpu.VMEM((C * C, K), F32),
            pltpu.VMEM((S, TI * C), BF16),
        ],
        compiler_params=pltpu.CompilerParams(vmem_limit_bytes=32 << 20),
        cost_estimate=pl.CostEstimate(flops=450_000_000, bytes_accessed=3_000_000, transcendentals=0),
    )(left_all, right_all, mask_j.astype(BF16), scaled, grad, right_keep, turn(right_give, "zb", 1), bias)

    got = lax.all_to_all(send, NEAR, 0, 0, tiled=True)
    total = jnp.sum(got[:, 32:72].astype(F32), axis=0)
    left_got = lax.dynamic_slice_in_dim(got, zb_at * 16, 16, 0)[:, :32]
    left_sum = jnp.sum(left_got.astype(F32), axis=0)
    left_mask = lax.dynamic_slice(mask, (col_at * 16, row_at * 8), (16, 8)).astype(BF16)
    bias_sum = total[32] + total[33]
    high = lax.reduce_precision(bias_sum, 8, 7)
    row = lax.broadcasted_iota(jnp.int32, (8, K), 0)
    bias_rows = jnp.where(row == 0, high[None], jnp.where(row == 1, (bias_sum - high)[None], 0.0))
    rows = jnp.concatenate([total[:32], bias_rows]).astype(BF16)
    send = jnp.concatenate(
        [right_part, jnp.broadcast_to(rows[None], (16, 40, K))], axis=1
    )
    got = lax.all_to_all(send, FAR, 0, 0, tiled=True)
    send, bias_sum = pl.pallas_call(
        join_kernel,
        out_shape=(
            jax.ShapeDtypeStruct((32, 48, K), BF16),
            jax.ShapeDtypeStruct((1, K), F32),
        ),
        in_specs=[VMEM],
        out_specs=(VMEM,) * 2,
        scratch_shapes=[pltpu.VMEM((32, K), F32)],
        compiler_params=pltpu.CompilerParams(vmem_limit_bytes=16 << 20),
    )(got)
    left_grad = pl.pallas_call(
        left_kernel,
        out_shape=jax.ShapeDtypeStruct((16, 8 * C), BF16),
        in_specs=[VMEM] * 2,
        out_specs=VMEM,
        compiler_params=pltpu.CompilerParams(vmem_limit_bytes=16 << 20),
    )(left_sum, left_mask)
    left_grad = left_grad.reshape(16, 8, C)
    bias_sum = bias_sum.reshape(K)
    got = lax.all_to_all(send, NEAR, 0, 0, tiled=True)
    right_mask = lax.dynamic_slice(mask, (row_at * 2, col_at * 64), (2, 64)).astype(F32)
    at = (zb_at * 16 + col_at).reshape(1).astype(jnp.int32)
    wout, right_grad = pl.pallas_call(
        tail_kernel,
        out_shape=(
            jax.ShapeDtypeStruct((C * C, K), F32),
            jax.ShapeDtypeStruct((2, C, 64), BF16),
        ),
        in_specs=[SMEM] + [VMEM] * 2,
        out_specs=(VMEM,) * 2,
        scratch_shapes=[pltpu.VMEM((2, C, 64), F32)],
        compiler_params=pltpu.CompilerParams(vmem_limit_bytes=16 << 20),
    )(at, got, right_mask)
    right_grad = right_grad.transpose(0, 2, 1)
    return left_grad, right_grad, wout, bias_sum


def solution(mesh):
    parts = Mesh(mesh.devices.reshape(SHAPE), NAMES)
    left_spec, right_spec = P(COL, ROW, None), P(ROW, COL, None)
    return jax.shard_map(
        per_device,
        mesh=parts,
        in_specs=(left_spec, right_spec, P(), P(ROW, COL, None), P()),
        out_specs=(left_spec, right_spec, P(), P()),
        check_vma=False,
    )
```

```python
import jax
import jax.numpy as jnp
from jax import lax
from jax.experimental import pallas as pl
from jax.experimental.pallas import tpu as pltpu
from jax.sharding import Mesh
from jax.sharding import PartitionSpec as P

SHAPE = (4, 2, 4, 2, 2, 4)
NAMES = ("zq", "zb", "yh", "core", "yl", "x")
ROW = ("zq", "zb", "yh", "core")
ZY = ("zq", "zb", "yh")
COL = ("yl", "x")
NEAR = ("zb", "core", "yl", "x")
FAR = ("zq", "yh")
C = 32
K = 128
S = 128
TI, TJ = 16, 32
F32, BF16 = jnp.float32, jnp.bfloat16
VMEM = pl.BlockSpec(memory_space=pltpu.VMEM)
SMEM = pl.BlockSpec(memory_space=pltpu.SMEM)


def dot(a, b, ca, cb):
    return lax.dot_general(a, b, (((ca,), (cb,)), ((), ())), preferred_element_type=F32)


def copies_kernel(l_ref, send_ref):
    left = l_ref[...].astype(F32)
    left = jnp.concatenate([left[:, i, :] for i in range(8)], axis=1).astype(BF16)
    for to in range(16):
        send_ref[to] = left


def turn_blocks(rows):
    half = [jnp.concatenate([rows[a][:, :64], rows[a + 2][:, :64]], axis=1) for a in range(2)]
    half += [jnp.concatenate([rows[a][:, 64:], rows[a + 2][:, 64:]], axis=1) for a in range(2)]
    turned = []
    for a, b in ((half[0], half[1]), (half[2], half[3])):
        for at in (0, 32):
            pieces = [x[:, y : y + 32] for y in (at, 64 + at) for x in (a, b)]
            turned.append(jnp.concatenate(pieces, axis=1))
    return turned


def scale_kernel(
    at_ref, keep_ref, take_ref, m_ref, mi_ref, mj_ref, w_ref, l_in,
    s_ref, bias_ref, g_ref, l_ref, rkeep_ref, rgive_ref, right_ref,
):
    keep, take = keep_ref[...], take_ref[...]
    first = at_ref[0] == 0
    pair = jnp.concatenate([jnp.where(first, keep, take), jnp.where(first, take, keep)])
    live = mi_ref[...][:, None, :] * mj_ref[...][None, :, :]
    live = live.reshape(TI * TJ, S).astype(BF16)
    counts = dot(live, jnp.ones((S, K), BF16), 1, 0)
    scaled = pair.reshape(TI * TJ, K).astype(F32) / jnp.maximum(counts, 1.0)
    total = jnp.sum(scaled, axis=0, keepdims=True)
    high = total.astype(BF16).astype(F32)
    row = lax.broadcasted_iota(jnp.int32, (16, K), 0)
    bias_ref[...] = jnp.where(row == 0, high, jnp.where(row == 1, total - high, 0.0)).astype(BF16)
    scaled = scaled.astype(BF16)
    s_ref[...] = scaled
    for g in range(C // 4):
        part = dot(w_ref[g * 4 * C : (g + 1) * 4 * C, :], scaled, 1, 1).astype(BF16)
        for i in range(TI):
            g_ref[i * C : (i + 1) * C, g * K : (g + 1) * K] = jnp.concatenate(
                [part[e * C : (e + 1) * C, i * TJ : (i + 1) * TJ] for e in range(4)], axis=1
            )
    lane = lax.broadcasted_iota(jnp.int32, (TI, TI * C), 1) // C
    spread = (lane == lax.broadcasted_iota(jnp.int32, (TI, TI * C), 0)).astype(BF16)
    live = dot(m_ref[...], spread, 1, 0).astype(BF16)
    for core in range(2):
        lanes = slice(core * 8 * C, (core + 1) * 8 * C)
        for col in range(8):
            rows = slice(col * 16, (col + 1) * 16)
            l_ref[rows, lanes] = l_in[core * 8 + col] * live[rows, lanes]
    right_ref[...] = dot(l_ref[...], g_ref[...], 1, 0).astype(BF16)
    zb = at_ref[1]
    for zq in range(4):
        at = zq * 32 + zb * 16
        rkeep_ref[zq] = right_ref[pl.ds(pl.multiple_of(at, 16), 16), :]
        at = zq * 32 + (1 - zb) * 16
        rgive_ref[zq] = right_ref[pl.ds(pl.multiple_of(at, 16), 16), :]


def main_kernel(
    l_ref, r_ref, m_ref, s_ref, g_ref, rkeep_ref, rtake_ref, bias_ref, send_ref, rsum_ref, o_ref, w_ref, left_ref
):
    for zq in range(4):
        total = rkeep_ref[zq].astype(F32) + rtake_ref[zq].astype(F32)
        for yh in range(4):
            rows = [total[yh * 4 : yh * 4 + 4, t * K : (t + 1) * K] for t in range(8)]
            rsum_ref[zq * 4 + yh] = jnp.concatenate(rows, axis=0).astype(BF16)
    right = r_ref[...] * jnp.concatenate([m_ref[...]] * C, axis=1)
    o_ref[...] = dot(l_ref[...], right, 0, 0).astype(BF16)
    pairs = s_ref[...]
    for g in range(C // 4):
        turned = [
            turn_blocks([o_ref[i * C : (i + 1) * C, g * K : (g + 1) * K] for i in range(b, b + 4)])
            for b in range(0, TI, 4)
        ]
        outer = [jnp.concatenate([blocks[e] for blocks in turned], axis=1) for e in range(4)]
        outer = jnp.concatenate(outer, axis=0)
        w_ref[g * 4 * C : (g + 1) * 4 * C, :] = dot(outer, pairs, 1, 0)
    for c in range(C):
        send_ref[c, 32:64, :] = w_ref[pl.ds(c, C, stride=C), :].astype(BF16)
        send_ref[c, 64:80, :] = bias_ref[...]
    left_ref[...] = dot(right, g_ref[...], 1, 1).astype(BF16)
    for zb in range(2):
        for core in range(2):
            for col in range(8):
                for h in range(2):
                    at = core * 8 * C + h * K
                    send_ref[zb * 16 + core * 8 + col, h * 16 : (h + 1) * 16, :] = left_ref[
                        col * 16 : (col + 1) * 16, at : at + K
                    ]


def join_kernel(got_ref, send_ref, bias_ref, total_ref):
    total = got_ref[0].astype(F32)
    for source in range(1, 16):
        total = total + got_ref[source].astype(F32)
    bias_ref[...] = jnp.sum(total[64:], axis=0, keepdims=True)
    rows = total[32:64].astype(BF16)
    total_ref[...] = total[:32]
    for core in range(2):
        right = [total_ref[pl.ds(core * 2 + q, 8, stride=4), :] for q in range(2)]
        right = jnp.concatenate(right, axis=0).astype(BF16)
        for zb in range(2):
            for col in range(8):
                to = zb * 16 + core * 8 + col
                send_ref[to, :32, :] = rows
                send_ref[to, 32:48, :] = right


def left_kernel(l_ref, ml_ref, left_ref):
    lane = lax.broadcasted_iota(jnp.int32, (8, 8 * C), 1) // C
    spread = (lane == lax.broadcasted_iota(jnp.int32, (8, 8 * C), 0)).astype(BF16)
    left = jnp.concatenate([l_ref[:16, :], l_ref[16:, :]], axis=1)
    left_ref[...] = (left * dot(ml_ref[...], spread, 1, 0)).astype(BF16)


def tail_kernel(at_ref, got_ref, m_ref, wout_ref, right_ref, turned_ref):
    for c in range(C):
        wout_ref[c * C : (c + 1) * C, :] = got_ref[c, :32, :].astype(F32)
    near, far = [got_ref[at_ref[0] + core * 8, 32:48, :].astype(F32) for core in range(2)]
    for q in range(2):
        for e in range(4):
            rows, lanes = slice(q * 8, (q + 1) * 8), slice(e * TJ, (e + 1) * TJ)
            piece = jnp.concatenate([near[rows, lanes], far[rows, lanes]], axis=1)
            turned_ref[q, pl.ds(e, 8, stride=4), :] = piece
    right_ref[...] = (turned_ref[...] * m_ref[...][:, None, :]).astype(BF16)


def turn(x, axis, by):
    n = SHAPE[NAMES.index(axis)]
    return lax.ppermute(x, axis, [(i, (i + by) % n) for i in range(n)])


def per_device(left, right, weight, pair, mask):
    row_at = lax.axis_index(ROW)
    zy_at = lax.axis_index(ZY)
    col_at = lax.axis_index(COL)
    core_at = lax.axis_index("core")
    zb_at = lax.axis_index("zb")
    send = pl.pallas_call(
        copies_kernel,
        out_shape=jax.ShapeDtypeStruct((16, 16, 8 * C), BF16),
        in_specs=[VMEM],
        out_specs=VMEM,
        compiler_params=pltpu.CompilerParams(vmem_limit_bytes=16 << 20),
    )(left)
    left_all = lax.all_to_all(send, ("core",) + COL, 0, 0, tiled=True)
    send = right.transpose(0, 2, 1).reshape(2, C, 2, TJ)
    send = send.transpose(2, 0, 1, 3).reshape(1, 2, 2, C * TJ)
    send = jnp.broadcast_to(send, (32, 2, 2, C * TJ)).reshape(64, 2, C * TJ)
    send, pair = lax.optimization_barrier((send, pair))
    right_all = lax.all_to_all(send, ROW, 0, 0, tiled=True).reshape(S, C * TJ)
    keep = lax.dynamic_slice_in_dim(pair, core_at * TJ, TJ, 1)
    give = lax.dynamic_slice_in_dim(pair, (1 - core_at) * TJ, TJ, 1)
    take = turn(give, "core", 1)
    mask_i = lax.dynamic_slice_in_dim(mask, zy_at * TI, TI, 1)
    mask_j = lax.dynamic_slice_in_dim(mask, col_at * 64 + core_at * TJ, TJ, 1)
    weight = weight.reshape(C, C, K).transpose(1, 0, 2).reshape(C * C, K)
    at = jnp.stack([core_at, zb_at]).astype(jnp.int32)

    scaled, bias, grad, left_all, right_keep, right_give = pl.pallas_call(
        scale_kernel,
        out_shape=(
            jax.ShapeDtypeStruct((TI * TJ, K), BF16),
            jax.ShapeDtypeStruct((16, K), BF16),
            jax.ShapeDtypeStruct((TI * C, C * TJ), BF16),
            jax.ShapeDtypeStruct((S, TI * C), BF16),
            jax.ShapeDtypeStruct((4, 16, C * TJ), BF16),
            jax.ShapeDtypeStruct((4, 16, C * TJ), BF16),
        ),
        in_specs=[SMEM] + [VMEM] * 7,
        out_specs=(VMEM,) * 6,
        scratch_shapes=[pltpu.VMEM((S, C * TJ), BF16)],
        compiler_params=pltpu.CompilerParams(vmem_limit_bytes=32 << 20),
        cost_estimate=pl.CostEstimate(flops=300_000_000, bytes_accessed=3_000_000, transcendentals=0),
    )(
        at, keep, take, mask_i.astype(BF16), mask_i.T.astype(F32), mask_j.T.astype(F32), weight, left_all
    )
    send, right_part = pl.pallas_call(
        main_kernel,
        out_shape=(
            jax.ShapeDtypeStruct((32, 80, K), BF16),
            jax.ShapeDtypeStruct((16, 32, K), BF16),
        ),
        in_specs=[VMEM] * 8,
        out_specs=(VMEM,) * 2,
        scratch_shapes=[
            pltpu.VMEM((TI * C, C * TJ), BF16),
            pltpu.VMEM((C * C, K), F32),
            pltpu.VMEM((S, TI * C), BF16),
        ],
        compiler_params=pltpu.CompilerParams(vmem_limit_bytes=32 << 20),
        cost_estimate=pl.CostEstimate(flops=450_000_000, bytes_accessed=3_000_000, transcendentals=0),
    )(left_all, right_all, mask_j.astype(BF16), scaled, grad, right_keep, turn(right_give, "zb", 1), bias)

    got = lax.all_to_all(send, NEAR, 0, 0, tiled=True)
    total = jnp.sum(got[:, 32:72].astype(F32), axis=0)
    left_got = lax.dynamic_slice_in_dim(got, zb_at * 16, 16, 0)[:, :32]
    left_sum = jnp.sum(left_got.astype(F32), axis=0)
    left_mask = lax.dynamic_slice(mask, (col_at * 16, row_at * 8), (16, 8)).astype(BF16)
    high = lax.reduce_precision(total[32:], 8, 7)
    rows = jnp.concatenate([total[:32], high, total[32:] - high]).astype(BF16)
    send = jnp.concatenate(
        [right_part, jnp.broadcast_to(rows[None], (16, 48, K))], axis=1
    )
    got = lax.all_to_all(send, FAR, 0, 0, tiled=True)
    send, bias_sum = pl.pallas_call(
        join_kernel,
        out_shape=(
            jax.ShapeDtypeStruct((32, 48, K), BF16),
            jax.ShapeDtypeStruct((1, K), F32),
        ),
        in_specs=[VMEM],
        out_specs=(VMEM,) * 2,
        scratch_shapes=[pltpu.VMEM((32, K), F32)],
        compiler_params=pltpu.CompilerParams(vmem_limit_bytes=16 << 20),
    )(got)
    left_grad = pl.pallas_call(
        left_kernel,
        out_shape=jax.ShapeDtypeStruct((16, 8 * C), BF16),
        in_specs=[VMEM] * 2,
        out_specs=VMEM,
        compiler_params=pltpu.CompilerParams(vmem_limit_bytes=16 << 20),
    )(left_sum, left_mask)
    left_grad = left_grad.reshape(16, 8, C)
    bias_sum = bias_sum.reshape(K)
    got = lax.all_to_all(send, NEAR, 0, 0, tiled=True)
    right_mask = lax.dynamic_slice(mask, (row_at * 2, col_at * 64), (2, 64)).astype(F32)
    at = (zb_at * 16 + col_at).reshape(1).astype(jnp.int32)
    wout, right_grad = pl.pallas_call(
        tail_kernel,
        out_shape=(
            jax.ShapeDtypeStruct((C * C, K), F32),
            jax.ShapeDtypeStruct((2, C, 64), BF16),
        ),
        in_specs=[SMEM] + [VMEM] * 2,
        out_specs=(VMEM,) * 2,
        scratch_shapes=[pltpu.VMEM((2, C, 64), F32)],
        compiler_params=pltpu.CompilerParams(vmem_limit_bytes=16 << 20),
    )(at, got, right_mask)
    right_grad = right_grad.transpose(0, 2, 1)
    return left_grad, right_grad, wout, bias_sum


def solution(mesh):
    parts = Mesh(mesh.devices.reshape(SHAPE), NAMES)
    left_spec, right_spec = P(COL, ROW, None), P(ROW, COL, None)
    return jax.shard_map(
        per_device,
        mesh=parts,
        in_specs=(left_spec, right_spec, P(), P(ROW, COL, None), P()),
        out_specs=(left_spec, right_spec, P(), P()),
        check_vma=False,
    )
```

```python
import jax
import jax.numpy as jnp
from jax import lax
from jax.experimental import pallas as pl
from jax.experimental.pallas import tpu as pltpu
from jax.sharding import Mesh
from jax.sharding import PartitionSpec as P

SHAPE = (4, 2, 4, 2, 2, 4)
NAMES = ("zq", "zb", "yh", "core", "yl", "x")
ROW = ("zq", "zb", "yh", "core")
ZY = ("zq", "zb", "yh")
COL = ("yl", "x")
NEAR = ("zb", "core", "yl", "x")
FAR = ("zq", "yh")
C = 32
K = 128
S = 128
TI, TJ = 16, 32
F32, BF16 = jnp.float32, jnp.bfloat16
VMEM = pl.BlockSpec(memory_space=pltpu.VMEM)
SMEM = pl.BlockSpec(memory_space=pltpu.SMEM)


def dot(a, b, ca, cb):
    return lax.dot_general(a, b, (((ca,), (cb,)), ((), ())), preferred_element_type=F32)


def copies_kernel(l_ref, send_ref):
    left = l_ref[...].astype(F32)
    left = jnp.concatenate([left[:, i, :] for i in range(8)], axis=1).astype(BF16)
    for to in range(16):
        send_ref[to] = left


def turn_blocks(rows):
    half = [jnp.concatenate([rows[a][:, :64], rows[a + 2][:, :64]], axis=1) for a in range(2)]
    half += [jnp.concatenate([rows[a][:, 64:], rows[a + 2][:, 64:]], axis=1) for a in range(2)]
    turned = []
    for a, b in ((half[0], half[1]), (half[2], half[3])):
        for at in (0, 32):
            pieces = [x[:, y : y + 32] for y in (at, 64 + at) for x in (a, b)]
            turned.append(jnp.concatenate(pieces, axis=1))
    return turned


def scale_kernel(
    at_ref, keep_ref, take_ref, m_ref, mi_ref, mj_ref, w_ref, l_in,
    s_ref, bias_ref, g_ref, l_ref, rkeep_ref, rgive_ref, right_ref,
):
    keep, take = keep_ref[...], take_ref[...]
    first = at_ref[0] == 0
    pair = jnp.concatenate([jnp.where(first, keep, take), jnp.where(first, take, keep)])
    live = mi_ref[...][:, None, :] * mj_ref[...][None, :, :]
    live = live.reshape(TI * TJ, S).astype(BF16)
    counts = dot(live, jnp.ones((S, K), BF16), 1, 0)
    scaled = pair.reshape(TI * TJ, K).astype(F32) / jnp.maximum(counts, 1.0)
    total = jnp.sum(scaled, axis=0, keepdims=True)
    high = total.astype(BF16).astype(F32)
    row = lax.broadcasted_iota(jnp.int32, (16, K), 0)
    bias_ref[...] = jnp.where(row == 0, high, jnp.where(row == 1, total - high, 0.0)).astype(BF16)
    scaled = scaled.astype(BF16)
    s_ref[...] = scaled
    for g in range(C // 4):
        part = dot(w_ref[g * 4 * C : (g + 1) * 4 * C, :], scaled, 1, 1).astype(BF16)
        for i in range(TI):
            g_ref[i * C : (i + 1) * C, g * K : (g + 1) * K] = jnp.concatenate(
                [part[e * C : (e + 1) * C, i * TJ : (i + 1) * TJ] for e in range(4)], axis=1
            )
    lane = lax.broadcasted_iota(jnp.int32, (TI, TI * C), 1) // C
    spread = (lane == lax.broadcasted_iota(jnp.int32, (TI, TI * C), 0)).astype(BF16)
    live = dot(m_ref[...], spread, 1, 0).astype(BF16)
    for core in range(2):
        lanes = slice(core * 8 * C, (core + 1) * 8 * C)
        for col in range(8):
            rows = slice(col * 16, (col + 1) * 16)
            l_ref[rows, lanes] = l_in[core * 8 + col] * live[rows, lanes]
    right_ref[...] = dot(l_ref[...], g_ref[...], 1, 0).astype(BF16)
    zb = at_ref[1]
    for zq in range(4):
        at = zq * 32 + zb * 16
        rkeep_ref[zq] = right_ref[pl.ds(pl.multiple_of(at, 16), 16), :]
        at = zq * 32 + (1 - zb) * 16
        rgive_ref[zq] = right_ref[pl.ds(pl.multiple_of(at, 16), 16), :]


def main_kernel(
    l_ref, r_ref, m_ref, s_ref, g_ref, rkeep_ref, rtake_ref, bias_ref, send_ref, rsum_ref, o_ref, w_ref
):
    for zq in range(4):
        total = rkeep_ref[zq].astype(F32) + rtake_ref[zq].astype(F32)
        for yh in range(4):
            rows = [total[yh * 4 : yh * 4 + 4, t * K : (t + 1) * K] for t in range(8)]
            rsum_ref[zq * 4 + yh] = jnp.concatenate(rows, axis=0).astype(BF16)
    right = r_ref[...] * jnp.concatenate([m_ref[...]] * C, axis=1)
    o_ref[...] = dot(l_ref[...], right, 0, 0).astype(BF16)
    pairs = s_ref[...]
    for g in range(C // 4):
        turned = [
            turn_blocks([o_ref[i * C : (i + 1) * C, g * K : (g + 1) * K] for i in range(b, b + 4)])
            for b in range(0, TI, 4)
        ]
        outer = [jnp.concatenate([blocks[e] for blocks in turned], axis=1) for e in range(4)]
        outer = jnp.concatenate(outer, axis=0)
        w_ref[g * 4 * C : (g + 1) * 4 * C, :] = dot(outer, pairs, 1, 0)
    for c in range(C):
        send_ref[c, 32:64, :] = w_ref[pl.ds(c, C, stride=C), :].astype(BF16)
        send_ref[c, 64:80, :] = bias_ref[...]
    left = dot(right, g_ref[...], 1, 1).astype(BF16)
    for zb in range(2):
        for core in range(2):
            for col in range(8):
                for h in range(2):
                    at = core * 8 * C + h * K
                    rows = left[col * 16 : (col + 1) * 16, at : at + K]
                    send_ref[zb * 16 + core * 8 + col, h * 16 : (h + 1) * 16, :] = rows


def join_kernel(got_ref, send_ref, bias_ref, total_ref):
    total = got_ref[0].astype(F32)
    for source in range(1, 16):
        total = total + got_ref[source].astype(F32)
    bias_ref[...] = jnp.sum(total[64:], axis=0, keepdims=True)
    rows = total[32:64].astype(BF16)
    total_ref[...] = total[:32]
    for core in range(2):
        right = [total_ref[pl.ds(core * 2 + q, 8, stride=4), :] for q in range(2)]
        right = jnp.concatenate(right, axis=0).astype(BF16)
        for zb in range(2):
            for col in range(8):
                to = zb * 16 + core * 8 + col
                send_ref[to, :32, :] = rows
                send_ref[to, 32:48, :] = right


def left_kernel(l_ref, ml_ref, left_ref):
    lane = lax.broadcasted_iota(jnp.int32, (8, 8 * C), 1) // C
    spread = (lane == lax.broadcasted_iota(jnp.int32, (8, 8 * C), 0)).astype(BF16)
    left = jnp.concatenate([l_ref[:16, :], l_ref[16:, :]], axis=1)
    left_ref[...] = (left * dot(ml_ref[...], spread, 1, 0)).astype(BF16)


def tail_kernel(at_ref, got_ref, m_ref, wout_ref, right_ref, turned_ref):
    for c in range(C):
        wout_ref[c * C : (c + 1) * C, :] = got_ref[c, :32, :].astype(F32)
    near, far = [got_ref[at_ref[0] + core * 8, 32:48, :].astype(F32) for core in range(2)]
    for q in range(2):
        for e in range(4):
            rows, lanes = slice(q * 8, (q + 1) * 8), slice(e * TJ, (e + 1) * TJ)
            piece = jnp.concatenate([near[rows, lanes], far[rows, lanes]], axis=1)
            turned_ref[q, pl.ds(e, 8, stride=4), :] = piece
    right_ref[...] = (turned_ref[...] * m_ref[...][:, None, :]).astype(BF16)


def turn(x, axis, by):
    n = SHAPE[NAMES.index(axis)]
    return lax.ppermute(x, axis, [(i, (i + by) % n) for i in range(n)])


def per_device(left, right, weight, pair, mask):
    row_at = lax.axis_index(ROW)
    zy_at = lax.axis_index(ZY)
    col_at = lax.axis_index(COL)
    core_at = lax.axis_index("core")
    zb_at = lax.axis_index("zb")
    send = pl.pallas_call(
        copies_kernel,
        out_shape=jax.ShapeDtypeStruct((16, 16, 8 * C), BF16),
        in_specs=[VMEM],
        out_specs=VMEM,
        compiler_params=pltpu.CompilerParams(vmem_limit_bytes=16 << 20),
    )(left)
    left_all = lax.all_to_all(send, ("core",) + COL, 0, 0, tiled=True)
    send = right.transpose(0, 2, 1).reshape(2, C, 2, TJ)
    send = send.transpose(2, 0, 1, 3).reshape(1, 2, 2, C * TJ)
    send = jnp.broadcast_to(send, (32, 2, 2, C * TJ)).reshape(64, 2, C * TJ)
    send, pair = lax.optimization_barrier((send, pair))
    right_all = lax.all_to_all(send, ROW, 0, 0, tiled=True).reshape(S, C * TJ)
    keep = lax.dynamic_slice_in_dim(pair, core_at * TJ, TJ, 1)
    give = lax.dynamic_slice_in_dim(pair, (1 - core_at) * TJ, TJ, 1)
    take = turn(give, "core", 1)
    mask_i = lax.dynamic_slice_in_dim(mask, zy_at * TI, TI, 1)
    mask_j = lax.dynamic_slice_in_dim(mask, col_at * 64 + core_at * TJ, TJ, 1)
    weight = weight.reshape(C, C, K).transpose(1, 0, 2).reshape(C * C, K)
    at = jnp.stack([core_at, zb_at]).astype(jnp.int32)

    scaled, bias, grad, left_all, right_keep, right_give = pl.pallas_call(
        scale_kernel,
        out_shape=(
            jax.ShapeDtypeStruct((TI * TJ, K), BF16),
            jax.ShapeDtypeStruct((16, K), BF16),
            jax.ShapeDtypeStruct((TI * C, C * TJ), BF16),
            jax.ShapeDtypeStruct((S, TI * C), BF16),
            jax.ShapeDtypeStruct((4, 16, C * TJ), BF16),
            jax.ShapeDtypeStruct((4, 16, C * TJ), BF16),
        ),
        in_specs=[SMEM] + [VMEM] * 7,
        out_specs=(VMEM,) * 6,
        scratch_shapes=[pltpu.VMEM((S, C * TJ), BF16)],
        compiler_params=pltpu.CompilerParams(vmem_limit_bytes=32 << 20),
        cost_estimate=pl.CostEstimate(flops=300_000_000, bytes_accessed=3_000_000, transcendentals=0),
    )(
        at, keep, take, mask_i.astype(BF16), mask_i.T.astype(F32), mask_j.T.astype(F32), weight, left_all
    )
    send, right_part = pl.pallas_call(
        main_kernel,
        out_shape=(
            jax.ShapeDtypeStruct((32, 80, K), BF16),
            jax.ShapeDtypeStruct((16, 32, K), BF16),
        ),
        in_specs=[VMEM] * 8,
        out_specs=(VMEM,) * 2,
        scratch_shapes=[
            pltpu.VMEM((TI * C, C * TJ), BF16),
            pltpu.VMEM((C * C, K), F32),
        ],
        compiler_params=pltpu.CompilerParams(vmem_limit_bytes=32 << 20),
        cost_estimate=pl.CostEstimate(flops=450_000_000, bytes_accessed=3_000_000, transcendentals=0),
    )(left_all, right_all, mask_j.astype(BF16), scaled, grad, right_keep, turn(right_give, "zb", 1), bias)

    got = lax.all_to_all(send, NEAR, 0, 0, tiled=True)
    total = jnp.sum(got[:, 32:72].astype(F32), axis=0)
    left_got = lax.dynamic_slice_in_dim(got, zb_at * 16, 16, 0)[:, :32]
    left_sum = jnp.sum(left_got.astype(F32), axis=0)
    left_mask = lax.dynamic_slice(mask, (col_at * 16, row_at * 8), (16, 8)).astype(BF16)
    high = lax.reduce_precision(total[32:], 8, 7)
    rows = jnp.concatenate([total[:32], high, total[32:] - high]).astype(BF16)
    send = jnp.concatenate(
        [right_part, jnp.broadcast_to(rows[None], (16, 48, K))], axis=1
    )
    got = lax.all_to_all(send, FAR, 0, 0, tiled=True)
    send, bias_sum = pl.pallas_call(
        join_kernel,
        out_shape=(
            jax.ShapeDtypeStruct((32, 48, K), BF16),
            jax.ShapeDtypeStruct((1, K), F32),
        ),
        in_specs=[VMEM],
        out_specs=(VMEM,) * 2,
        scratch_shapes=[pltpu.VMEM((32, K), F32)],
        compiler_params=pltpu.CompilerParams(vmem_limit_bytes=16 << 20),
    )(got)
    left_grad = pl.pallas_call(
        left_kernel,
        out_shape=jax.ShapeDtypeStruct((16, 8 * C), BF16),
        in_specs=[VMEM] * 2,
        out_specs=VMEM,
        compiler_params=pltpu.CompilerParams(vmem_limit_bytes=16 << 20),
    )(left_sum, left_mask)
    left_grad = left_grad.reshape(16, 8, C)
    bias_sum = bias_sum.reshape(K)
    got = lax.all_to_all(send, NEAR, 0, 0, tiled=True)
    right_mask = lax.dynamic_slice(mask, (row_at * 2, col_at * 64), (2, 64)).astype(F32)
    at = (zb_at * 16 + col_at).reshape(1).astype(jnp.int32)
    wout, right_grad = pl.pallas_call(
        tail_kernel,
        out_shape=(
            jax.ShapeDtypeStruct((C * C, K), F32),
            jax.ShapeDtypeStruct((2, C, 64), BF16),
        ),
        in_specs=[SMEM] + [VMEM] * 2,
        out_specs=(VMEM,) * 2,
        scratch_shapes=[pltpu.VMEM((2, C, 64), F32)],
        compiler_params=pltpu.CompilerParams(vmem_limit_bytes=16 << 20),
    )(at, got, right_mask)
    right_grad = right_grad.transpose(0, 2, 1)
    return left_grad, right_grad, wout, bias_sum


def solution(mesh):
    parts = Mesh(mesh.devices.reshape(SHAPE), NAMES)
    left_spec, right_spec = P(COL, ROW, None), P(ROW, COL, None)
    return jax.shard_map(
        per_device,
        mesh=parts,
        in_specs=(left_spec, right_spec, P(), P(ROW, COL, None), P()),
        out_specs=(left_spec, right_spec, P(), P()),
        check_vma=False,
    )
```
